512 devices in a mesh: vocab: 64 (over y, z_lo, core), batch: 8 (over z_hi, x).
Axes of the slice: x: 4, y: 8, z: 8 (z_hi: 2, z_lo: 4; z = z_hi * 4 + z_lo), core: 2. Of those that a mesh axis runs over, the one named last changes fastest.
Arguments:
- latent_states: bfloat16 [128, 5, 16384], P('vocab', None, 'batch'), may hold values from -150 to 150
- unembedding_weights: bfloat16 [16384, 8, 64, 128], P('batch', None, 'vocab'), may hold values from -0.046875 to 0.046875
- drafter_raw_scores: bfloat16 [128, 5, 8, 64, 128], P('vocab', None, 'batch'), may hold values from -16 to 160
- sampler_heat: float32 [128], P('batch'), may hold values from 0.7 to 1.4
- drafter_guesses: int32 [128, 5], P('batch'), may hold values from 0 to 65535
- first_refused_slot: int32 [128], P('batch'), may hold values from 0 to 4
Outputs:
- ratio: float32 [128, 5], P('batch')
- residual: bfloat16 [128, 8, 64, 128], P('batch', None, 'vocab')
The draws below stay inside these ranges and needn't reach their ends.
All inputs are finite; a program needn't handle non-finite values.
Results may differ from the reference program's by a relative error of at most 0.01105.
Values may be sent and summed in bfloat16 or wider, within the bound.
A program may use at most 64 MiB of HBM per device.

```python
import math
import jax
import jax.numpy as jnp

D = 16384
LANE = 128
POS = 5
QUERY_COUNT_ALL = 128
VOCAB = 65536
N_VOCAB = 64
N_BATCH = 8


def draw_latent_states(key, part):
    key = jax.random.fold_in(key, 11)
    array_shape = (QUERY_COUNT_ALL, POS, D)
    values = 3.5 * jax.random.truncated_normal(key, -4.0, 4.0, array_shape, jnp.float32)
    return values.astype(jnp.bfloat16)


def draw_drafter_raw_scores(key, part):
    key = jax.random.fold_in(key, 23)
    array_shape = (QUERY_COUNT_ALL, POS, VOCAB)
    values = 3.5 * jax.random.truncated_normal(key, -4.0, 4.0, array_shape, jnp.float32)
    return values.reshape(QUERY_COUNT_ALL, POS, N_BATCH, N_VOCAB, LANE).astype(jnp.bfloat16)


def touch_ends(drawn, own_key, low, top_value):
    longest = drawn.shape.index(max(drawn.shape))
    spots = []
    for shift in (0, 1):
        where = [jax.random.randint(jax.random.fold_in(own_key, axis), (), 0, length) for axis, length in enumerate(drawn.shape)]
        where[longest] = (where[longest] + shift) % drawn.shape[longest]
        spots.append(tuple(where))
    return drawn.at[spots[0]].set(low).at[spots[1]].set(top_value)


def levels(rng, shape, cuts, low, top_value):
    level, own = 1.0, jax.random.fold_in(rng, 6)
    for axis_at, parts in cuts:
        draws = jnp.exp(jax.random.uniform(jax.random.fold_in(own, axis_at), (parts,), jnp.float32, low / len(cuts), top_value / len(cuts)))
        level = level * jnp.repeat(draws, shape[axis_at] // parts).reshape([-1 if axis == axis_at else 1 for axis in range(len(shape))])
    return level


def bell_draw(key, extent, scale, bound, shards=(), held_as=jnp.bfloat16):
    gain = levels(key, extent, shards, -0.22, 0.18) if shards else 1.0
    array = jax.random.normal(key, extent, jnp.float32) * scale * gain
    return jnp.minimum(jnp.maximum(array, -bound), bound).astype(held_as)


def setup_inputs(seed: int = 0) -> dict:
    key_list = jax.random.split(jax.random.key(seed), 7)
    return {
        "latent_states": draw_latent_states(jax.random.fold_in(key_list[6], 71), 0),
        "unembedding_weights": bell_draw(key_list[1], (D, N_BATCH, N_VOCAB, LANE), D ** -0.5, 0.046875, ((0, 8), (2, 64))),
        "drafter_raw_scores": draw_drafter_raw_scores(jax.random.fold_in(key_list[6], 71), 0),
        "sampler_heat": jnp.clip(jnp.exp(math.log(1.4) - 0.6931472 * jax.random.uniform(key_list[3], (QUERY_COUNT_ALL,), jnp.float32) ** levels(key_list[3], (QUERY_COUNT_ALL,), ((0, 8),), -0.2, 0.2)), 0.7, 1.4),
        "drafter_guesses": touch_ends(jax.random.randint(key_list[4], (QUERY_COUNT_ALL, POS), 0, VOCAB), jax.random.fold_in(key_list[4], 1), 0, VOCAB - 1).astype(jnp.int32),
        "first_refused_slot": touch_ends(jax.random.randint(key_list[5], (QUERY_COUNT_ALL,), 0, POS), jax.random.fold_in(key_list[5], 1), 0, POS - 1).astype(jnp.int32),
    }


def reference(latent_states, unembedding_weights, drafter_raw_scores, sampler_heat, drafter_guesses, first_refused_slot):
    rows = latent_states.reshape(QUERY_COUNT_ALL * POS, D)
    logits = jnp.dot(rows, unembedding_weights.reshape(D, VOCAB), preferred_element_type=jnp.float32)
    multiplier = sampler_heat[:, None, None]
    target_scores = logits.reshape(QUERY_COUNT_ALL, POS, VOCAB) / multiplier
    draft_scores = drafter_raw_scores.astype(jnp.float32).reshape(QUERY_COUNT_ALL, POS, VOCAB) / multiplier
    target_max = jnp.max(target_scores, axis=-1)
    draft_max = jnp.max(draft_scores, axis=-1)
    target_exp = jnp.exp(target_scores - target_max[..., None])
    draft_exp = jnp.exp(draft_scores - draft_max[..., None])
    target_total = jnp.sum(target_exp, axis=-1)
    draft_total = jnp.sum(draft_exp, axis=-1)
    target_prob = target_exp / target_total[..., None]
    draft_prob = draft_exp / draft_total[..., None]
    target_token = jnp.take_along_axis(target_scores, drafter_guesses[..., None], axis=-1)[..., 0]
    draft_token = jnp.take_along_axis(draft_scores, drafter_guesses[..., None], axis=-1)[..., 0]
    target_log = target_token - target_max - jnp.log(target_total)
    draft_log = draft_token - draft_max - jnp.log(draft_total)
    ratio = jnp.exp(jnp.minimum(0.0, target_log - draft_log))
    index = first_refused_slot[:, None, None].astype(jnp.int32)
    target_stop = jnp.take_along_axis(target_prob, index, axis=1)[:, 0]
    draft_stop = jnp.take_along_axis(draft_prob, index, axis=1)[:, 0]
    excess = jnp.maximum(target_stop - draft_stop, 0.0) + 0.0625 * target_stop
    residual = excess / jnp.sum(excess, axis=-1, keepdims=True)
    residual = residual.astype(jnp.bfloat16).reshape(QUERY_COUNT_ALL, N_BATCH, N_VOCAB, LANE)
    return ratio, residual
```

```python
import jax
import jax.numpy as jnp
from jax import lax
from jax.experimental import pallas as pl
from jax.experimental.pallas import tpu as pltpu
from jax.sharding import PartitionSpec as P

blend_share = 0.0625

RING_Y = 8
GROUP = 8
RING_X = 4
REQ = 2
POS = 5
LANE = 128
MESH = pl.DeviceIdType.MESH
OFFSETS = ((0,), (-1, 1), (-2, 2), (-3, 3), (4,))


def kernel(
    x_ref,
    w_hbm,
    d_ref,
    meta_ref,
    ratio_ref,
    resid_ref,
    w_raw,
    w_mat,
    z_in,
    g,
    part,
    relay_in,
    root_in,
    cross_in,
    a1,
    a2,
    a3,
    ts,
    ds,
    st_out,
    st_in,
    w_sem,
    z_send,
    z_recv,
    y_send,
    y_recv,
    sib_send,
    sib_recv,
    p_send,
    relay_recv,
    root_recv,
    cross_recv,
    a_send,
    a_recv,
    st_send,
    st_recv,
):
    v = lax.axis_index("vocab")
    b = lax.axis_index("batch")
    y = v // GROUP
    place = v % GROUP
    core = place % 2
    x = b % RING_X
    zh = b // RING_X
    depth = w_raw.shape[0]
    chunks = x_ref.shape[1]
    half_chunks = chunks // 2
    rows = meta_ref.shape[0]
    outer = w_raw.shape[1]
    columns = outer * LANE
    half = columns // 2
    queries = rows // POS

    def at(y_, place_, b_):
        return (y_ * GROUP + place_, b_)

    def remote(src, dst, send, recv, device):
        return pltpu.make_async_remote_copy(
            src_ref=src,
            dst_ref=dst,
            send_sem=send,
            recv_sem=recv,
            device_id=device,
            device_id_type=MESH,
        )

    def await_bytes(ref, sem):
        pltpu.make_async_copy(ref, ref, sem).wait()

    w_copy = pltpu.make_async_copy(w_hbm, w_raw, w_sem)
    w_copy.start()

    barrier = pltpu.get_barrier_semaphore()
    for t in range(1, 8):
        pl.semaphore_signal(
            barrier, inc=1, device_id=at(y, (place + t) % GROUP, b), device_id_type=MESH
        )
        pl.semaphore_signal(
            barrier, inc=1, device_id=at((y + t) % RING_Y, place, b), device_id_type=MESH
        )
        pl.semaphore_signal(
            barrier, inc=1, device_id=at(y, place, (b + t) % 8), device_id_type=MESH
        )
    pl.semaphore_wait(barrier, 21)

    for t in range(1, 8):
        to = (place + t) % GROUP
        first = (to % 2) * half_chunks
        remote(
            x_ref.at[:, pl.ds(first, half_chunks)],
            z_in.at[place],
            z_send,
            z_recv,
            at(y, to, b),
        ).start()
    pltpu.make_async_copy(
        x_ref.at[:, pl.ds(core * half_chunks, half_chunks)], z_in.at[place], z_recv
    ).start()

    for t in range(1, 8):
        to = (place + t) % GROUP
        remote(
            d_ref.at[:, to], a1.at[place], a_send.at[0], a_recv.at[0], at(y, to, b)
        ).start()
    pltpu.make_async_copy(d_ref.at[:, place], a1.at[place], a_recv.at[0]).start()

    w_copy.wait()
    fold = 64

    @pl.loop(0, depth // fold)
    def _(i):
        f = pl.multiple_of(i * fold, fold)
        w_mat[pl.ds(f, fold), :] = w_raw[pl.ds(f, fold)].reshape(fold, columns)

    def mine(yy):
        return g.at[yy, pl.ds(core * half_chunks, half_chunks)]

    def to_sibling(yy, k):
        remote(
            mine(yy), mine(yy), sib_send.at[k], sib_recv.at[k], at(y, place + 1 - 2 * core, b)
        ).start()

    def theirs(yy):
        return g.at[yy, pl.ds((1 - core) * half_chunks, half_chunks)]

    def wait_sibling(yy, k):
        await_bytes(theirs(yy), sib_recv.at[k])

    right = at((y + 1) % RING_Y, place, b)
    left = at((y + RING_Y - 1) % RING_Y, place, b)

    def around(o):
        return (y + o + RING_Y) % RING_Y

    await_bytes(z_in, z_recv)
    for s in range(half_chunks):
        g[y, core * half_chunks + s] = jnp.swapaxes(z_in[:, :, s], 0, 1).reshape(rows, LANE)
    remote(mine(y), mine(y), y_send.at[0, 0], y_recv.at[0, 0], right).start()
    remote(mine(y), mine(y), y_send.at[1, 0], y_recv.at[1, 0], left).start()
    to_sibling(y, 0)

    await_bytes(a1, a_recv.at[0])
    for t in range(1, 8):
        to = (y + t) % RING_Y
        remote(
            a1.at[:, to], a2.at[y], a_send.at[1], a_recv.at[1], at(to, place, b)
        ).start()
    pltpu.make_async_copy(a1.at[:, y], a2.at[y], a_recv.at[1]).start()

    quarter = half_chunks // 2

    def sub(yy, direction):
        return g.at[yy, pl.ds(core * half_chunks + direction * quarter, quarter)]

    def ring_step(t):
        if t < 4:
            for direction, to in ((0, right), (1, left)):
                yy = around(-t if direction == 0 else t)
                await_bytes(mine(yy), y_recv.at[direction, t - 1])
                piece = mine(yy) if t < 3 else sub(yy, direction)
                remote(
                    piece, piece, y_send.at[direction, t], y_recv.at[direction, t], to
                ).start()
                to_sibling(yy, 2 * t - 1 + direction)
        else:
            yy = around(4)
            for direction in (0, 1):
                await_bytes(sub(yy, direction), y_recv.at[direction, 3])
            to_sibling(yy, 7)

    def multiply(blocks):
        span = 256
        for n in range(columns // span):
            acc = None
            for kk in range(depth // 256):
                lhs = jnp.concatenate(
                    [
                        jnp.concatenate([g[yy, 2 * kk], g[yy, 2 * kk + 1]], axis=1)
                        for yy in blocks
                    ],
                    axis=0,
                )
                term = jnp.dot(
                    lhs,
                    w_mat[kk * 256 : (kk + 1) * 256, n * span : (n + 1) * span],
                    preferred_element_type=jnp.float32,
                )
                acc = term if acc is None else acc + term
            at_half, col = (n * span) // half, (n * span) % half
            for i, yy in enumerate(blocks):
                part[yy, at_half, :, col : col + span] = acc[i * rows : (i + 1) * rows]

    def roles(yy):
        xd = yy % RING_X
        return xd, (x - xd + RING_X) % RING_X, yy // RING_X

    def reduce_a(yy):
        xd, d, rk = roles(yy)

        @pl.when(d == 2)
        def _():
            for h, nb in ((0, (xd + 1) % RING_X), (1, (xd + 3) % RING_X)):
                remote(
                    part.at[yy, h],
                    relay_in.at[yy],
                    p_send.at[yy, h],
                    relay_recv.at[yy],
                    (v, zh * RING_X + nb),
                ).start()

        @pl.when(d % 2 == 1)
        def _():
            side = d // 2
            remote(
                part.at[yy, 1 - side],
                root_in.at[rk, side, 1 - side],
                p_send.at[yy, 1 - side],
                root_recv.at[rk, side, 1 - side],
                (v, zh * RING_X + xd),
            ).start()

    def reduce_b(yy):
        xd, d, rk = roles(yy)

        @pl.when(d % 2 == 1)
        def _():
            side = d // 2
            await_bytes(relay_in.at[yy], relay_recv.at[yy])
            part[yy, side] = part[yy, side] + relay_in[yy]
            remote(
                part.at[yy, side],
                root_in.at[rk, side, side],
                p_send.at[yy, side],
                root_recv.at[rk, side, side],
                (v, zh * RING_X + xd),
            ).start()

    def reduce_c(yy):
        xd, d, rk = roles(yy)

        @pl.when(d == 0)
        def _():
            for h in (0, 1):
                await_bytes(root_in.at[rk, 1 - h, h], root_recv.at[rk, 1 - h, h])
                await_bytes(root_in.at[rk, h, h], root_recv.at[rk, h, h])
                part[yy, h] = part[yy, h] + root_in[rk, 0, h] + root_in[rk, 1, h]

                @pl.when(rk != zh)
                def _():
                    remote(
                        part.at[yy, h],
                        cross_in.at[h],
                        p_send.at[yy, h],
                        cross_recv.at[h],
                        (v, rk * RING_X + x),
                    ).start()

    heat = meta_ref[:, 0:1]
    guess = meta_ref[:, 1:2].astype(jnp.int32)
    stop = meta_ref[:, 2:3]
    lane_ids = lax.broadcasted_iota(jnp.int32, (rows, LANE), 1)

    def statistics(scores):
        top = scores[0]
        for o in range(1, outer):
            top = jnp.maximum(top, scores[o])
        top = jnp.max(top, axis=1, keepdims=True)
        total = jnp.zeros((rows, LANE), jnp.float32)
        hit = jnp.zeros((rows, LANE), jnp.float32)
        for o in range(outer):
            value = scores[o]
            total = total + jnp.exp(value - top)
            ids = (o * (RING_Y * GROUP) + v) * LANE + lane_ids
            hit = hit + jnp.where(ids == guess, value, 0.0)
        return (
            top,
            jnp.sum(total, axis=1, keepdims=True),
            jnp.sum(hit, axis=1, keepdims=True),
        )

    def draft_scores():
        await_bytes(a3, a_recv.at[2])
        for o in range(outer):
            logits = jnp.swapaxes(a3[o], 0, 1).reshape(rows, LANE).astype(jnp.float32)
            ds[o] = logits / heat
        return statistics(ds)

    def draft_step_3():
        await_bytes(a2, a_recv.at[1])
        for t in range(1, 8):
            to = (b + t) % 8
            remote(a2.at[to], a3.at[b], a_send.at[2], a_recv.at[2], at(y, place, to)).start()
        pltpu.make_async_copy(a2.at[b], a3.at[b], a_recv.at[2]).start()

    ring_step(1)
    wait_sibling(y, 0)
    multiply((y,))
    reduce_a(y)
    draft_step_3()

    ring_step(2)
    wait_sibling(around(-1), 1)
    wait_sibling(around(1), 2)
    multiply((around(-1), around(1)))
    reduce_a(around(-1))
    reduce_a(around(1))
    reduce_b(y)

    ring_step(3)
    wait_sibling(around(-2), 3)
    wait_sibling(around(2), 4)
    multiply((around(-2), around(2)))
    reduce_a(around(-2))
    reduce_a(around(2))
    reduce_b(around(-1))
    reduce_b(around(1))
    reduce_c(y)

    ring_step(4)
    wait_sibling(around(-3), 5)
    wait_sibling(around(3), 6)
    multiply((around(-3), around(3)))
    reduce_a(around(-3))
    reduce_a(around(3))
    reduce_b(around(-2))
    reduce_b(around(2))
    reduce_c(around(-1))
    reduce_c(around(1))

    wait_sibling(around(4), 7)
    multiply((around(4),))
    reduce_a(around(4))
    reduce_b(around(-3))
    reduce_b(around(3))
    reduce_c(around(-2))
    reduce_c(around(2))
    reduce_b(around(4))
    reduce_c(around(-3))
    reduce_c(around(3))
    d_top, d_total, d_hit = draft_scores()
    reduce_c(around(4))

    for h in (0, 1):
        await_bytes(cross_in.at[h], cross_recv.at[h])
        for i in range(outer // 2):
            span = slice(i * LANE, (i + 1) * LANE)
            ts[h * (outer // 2) + i] = (part[b, h, :, span] + cross_in[h, :, span]) / heat
    t_top, t_total, t_hit = statistics(ts)

    def spread(k, hop):
        me = (place, y)[hop]
        for t in range(1, 8):
            to = (me + t) % 8
            remote(
                st_out.at[k],
                st_in.at[k, me],
                st_send.at[k],
                st_recv.at[k],
                at(y, to, b) if hop == 0 else at(to, place, b),
            ).start()
        pltpu.make_async_copy(st_out.at[k], st_in.at[k, me], st_recv.at[k]).start()
        await_bytes(st_in.at[k], st_recv.at[k])

    wide = jnp.zeros((rows, LANE), jnp.float32)
    for i, column in enumerate((t_top, t_total, t_hit, d_top, d_total, d_hit)):
        wide = jnp.where(lane_ids == i, column, wide)
    wide = jnp.concatenate([wide, jnp.ones((LANE - rows, LANE), jnp.float32)], axis=0)
    st_out[0] = jnp.transpose(wide)[0:8]

    def merged(k):
        out = []
        for i in (0, 3):
            top = st_in[k, 0, i : i + 1]
            for j in range(1, 8):
                top = jnp.maximum(top, st_in[k, j, i : i + 1])
            total = jnp.zeros_like(top)
            hit = jnp.zeros_like(top)
            for j in range(8):
                total = total + st_in[k, j, i + 1 : i + 2] * jnp.exp(
                    st_in[k, j, i : i + 1] - top
                )
                hit = hit + st_in[k, j, i + 2 : i + 3]
            out += [top, total, hit]
        return out

    spread(0, 0)
    for i, value in enumerate(merged(0)):
        st_out[1, i : i + 1] = value
    st_out[1, 6:8] = jnp.zeros((2, LANE), jnp.float32)
    spread(1, 1)
    t_max, t_sum, t_tok, d_max, d_sum, d_tok = merged(1)

    def chosen(block):
        out = None
        for p in range(POS):
            mask = stop[p * queries : (p + 1) * queries] > 0.5
            value = block(p)
            picked = jnp.where(mask, value, 0.0)
            out = picked if out is None else out + picked
        return out

    def rows_of(p):
        return slice(p * queries, (p + 1) * queries)

    filler = jnp.zeros((LANE - 4, LANE), jnp.float32)
    tall = jnp.transpose(jnp.concatenate([t_max, t_sum, d_max, d_sum, filler], axis=0))
    picks = chosen(lambda p: tall[rows_of(p)])
    tm, tt, dm, dt = (picks[:, i : i + 1] for i in range(4))
    sums = jnp.zeros((queries, LANE), jnp.float32)
    excesses = []
    for o in range(outer):
        t_stop = jnp.exp(chosen(lambda p: ts[o, rows_of(p)]) - tm) / tt
        d_stop = jnp.exp(chosen(lambda p: ds[o, rows_of(p)]) - dm) / dt
        excess = jnp.maximum(t_stop - d_stop, 0.0) + blend_share * t_stop
        sums = sums + excess
        excesses.append(excess)
    sums = jnp.broadcast_to(jnp.sum(sums, axis=1, keepdims=True), (queries, LANE))
    sums = jnp.concatenate([sums, jnp.zeros((LANE - queries, LANE), jnp.float32)], axis=0)
    st_out[2] = jnp.transpose(sums)[0:8]
    spread(2, 0)
    total = st_in[2, 0]
    for j in range(1, 8):
        total = total + st_in[2, j]
    st_out[3] = total
    spread(3, 1)
    total = st_in[3, 0]
    for j in range(1, 8):
        total = total + st_in[3, j]
    total = jnp.concatenate([total, jnp.zeros((LANE - 8, LANE), jnp.float32)], axis=0)
    total = jnp.transpose(total)[0:queries, 0:1]
    for o in range(outer):
        resid_ref[:, o * LANE : (o + 1) * LANE] = (excesses[o] / total).astype(jnp.bfloat16)

    t_log = t_tok - t_max - jnp.log(t_sum)
    d_log = d_tok - d_max - jnp.log(d_sum)
    ratio_ref[...] = jnp.broadcast_to(
        jnp.exp(jnp.minimum(0.0, t_log - d_log)), ratio_ref.shape
    )

    await_bytes(z_in.at[pl.ds(0, 7)], z_send)
    for k, buffer in enumerate((a1, a2, a3)):
        await_bytes(buffer.at[pl.ds(0, 7)], a_send.at[k])
    for k in range(4):
        await_bytes(st_in.at[k, pl.ds(0, 7)], st_send.at[k])
    for direction in (0, 1):
        for t in range(4):
            piece = mine(y) if t < 3 else sub(y, direction)
            await_bytes(piece, y_send.at[direction, t])
    for k in range(8):
        await_bytes(mine(y), sib_send.at[k])
    for t in range(1, 8):
        yy = (b + t) % 8
        for h in (0, 1):
            await_bytes(part.at[yy, h], p_send.at[yy, h])


def per_device(
    latent_states,
    unembedding_weights,
    drafter_raw_scores,
    sampler_heat,
    drafter_guesses,
    first_refused_slot,
):
    depth = latent_states.shape[2]
    outer = unembedding_weights.shape[1]
    columns = outer * LANE
    chunks = depth // LANE
    queries = sampler_heat.shape[0]
    rows = queries * POS
    own = latent_states.reshape(REQ, POS, chunks, LANE).transpose(1, 2, 0, 3)
    weights = unembedding_weights.reshape(depth, outer, LANE)
    draft = drafter_raw_scores.reshape(REQ, POS, RING_Y, GROUP, LANE).transpose(2, 3, 1, 0, 4)
    steps = lax.broadcasted_iota(jnp.int32, (POS, queries), 0)
    meta = jnp.stack(
        [
            jnp.broadcast_to(sampler_heat[None, :], (POS, queries)),
            drafter_guesses.T.astype(jnp.float32),
            (steps == first_refused_slot[None, :]).astype(jnp.float32),
        ],
        axis=-1,
    ).reshape(rows, 3)
    meta = jnp.pad(meta, ((0, 0), (0, LANE - 3)))
    f32, bf16 = jnp.float32, jnp.bfloat16
    dma = pltpu.SemaphoreType.DMA
    half = columns // 2
    ratio, residual = pl.pallas_call(
        kernel,
        out_shape=(
            jax.ShapeDtypeStruct((8, LANE), f32),
            jax.ShapeDtypeStruct((queries, columns), bf16),
        ),
        in_specs=[
            pl.BlockSpec(memory_space=pltpu.VMEM),
            pl.BlockSpec(memory_space=pl.ANY),
            pl.BlockSpec(memory_space=pltpu.VMEM),
            pl.BlockSpec(memory_space=pltpu.VMEM),
        ],
        out_specs=(
            pl.BlockSpec(memory_space=pltpu.VMEM),
            pl.BlockSpec(memory_space=pltpu.VMEM),
        ),
        scratch_shapes=[
            pltpu.VMEM((depth, outer, LANE), bf16),
            pltpu.VMEM((depth, columns), bf16),
            pltpu.VMEM((GROUP, POS, chunks // 2, REQ, LANE), bf16),
            pltpu.VMEM((RING_Y, chunks, rows, LANE), bf16),
            pltpu.VMEM((RING_Y, 2, rows, half), f32),
            pltpu.VMEM((RING_Y, rows, half), f32),
            pltpu.VMEM((2, 2, 2, rows, half), f32),
            pltpu.VMEM((2, rows, half), f32),
            pltpu.VMEM((GROUP, RING_Y, POS, REQ, LANE), bf16),
            pltpu.VMEM((RING_Y, GROUP, POS, REQ, LANE), bf16),
            pltpu.VMEM((8, GROUP, POS, REQ, LANE), bf16),
            pltpu.VMEM((outer, rows, LANE), f32),
            pltpu.VMEM((outer, rows, LANE), f32),
            pltpu.VMEM((4, 8, LANE), f32),
            pltpu.VMEM((4, 8, 8, LANE), f32),
            dma,
            dma,
            dma,
            dma((2, 4)),
            dma((2, 4)),
            dma((8,)),
            dma((8,)),
            dma((8, 2)),
            dma((8,)),
            dma((2, 2, 2)),
            dma((2,)),
            dma((3,)),
            dma((3,)),
            dma((4,)),
            dma((4,)),
        ],
        compiler_params=pltpu.CompilerParams(
            collective_id=0, has_side_effects=True, vmem_limit_bytes=48 << 20
        ),
    )(own, weights, draft, meta)
    ratio = ratio[0, :rows].reshape(POS, queries).T
    residual = residual.reshape(queries, outer, 1, LANE)
    return ratio, residual


def solution(mesh):
    in_specs = (
        P("vocab", None, "batch"),
        P("batch", None, "vocab", None),
        P("vocab", None, "batch", None, None),
        P("batch"),
        P("batch", None),
        P("batch"),
    )
    out_specs = (P("batch", None), P("batch", None, "vocab", None))
    return jax.shard_map(
        per_device, mesh=mesh, in_specs=in_specs, out_specs=out_specs, check_vma=False
    )
```
